256 devices in a mesh: sec: 2 (over y_hi), dp: 16 (over y_lo, x, core), mp: 8 (over z).
Axes of the slice: x: 4, y: 4 (y_hi: 2, y_lo: 2; y = y_hi * 2 + y_lo), z: 8, core: 2. Of those that a mesh axis runs over, the one named last changes fastest.
Arguments:
- hidden_pre: bfloat16 [16384, 12288], P('dp', 'mp'), may hold values from -6 to 6
- residual: bfloat16 [16384, 3072], P('dp', 'mp'), may hold values from -64 to 64
- w_down: bfloat16 [3072, 12288], P('dp', 'mp'), may hold values from -0.0546875 to 0.0546875
- head_weight: bfloat16 [3072, 4096], P('dp', 'mp'), may hold values from -0.109375 to 0.109375
- norm_gain: float32 [3072], replicated, may hold values from 0.5 to 1.5
- segment_logits: bfloat16 [2, 16384, 4096], P('sec', ('dp', 'mp')), may hold values from -64 to 320
- student_hidden: bfloat16 [16384, 1024], P(('dp', 'mp')), may hold values from -24 to 24
- frame_mask: int32 [16384], P(('dp', 'mp')), may hold values 0 or 1
Outputs:
- segment_out: bfloat16 [2, 16384, 4096], P('sec', ('dp', 'mp'))
- grad_out: float32 [2, 1024, 4096], P('sec', ('dp', 'mp'))
The draws below stay inside these ranges and needn't reach their ends.
All inputs are finite; a program needn't handle non-finite values. No bound on the sum of `frame_mask` on one device may be relied on, other than what follows from the above.
Results may differ from the reference program's by a relative error of at most 0.015.
Values may be sent and summed in bfloat16 or wider, within the bound.
No kernel may reach another device: no remote copies, remote signals or barrier semaphores. Data moves between devices by JAX's collectives and lax.ppermute only.
A program may use at most 128 MiB of HBM per device.

```python
import math
import jax
import jax.numpy as jnp
from jax import lax

DT = 3072
FF = 12288
VOCAB = 4096
DS = 1024
TOKENS = 16384
N_MP = 8


def draw_segment_logits(key, part):
    key = jax.random.fold_in(key, 11)
    keys = jax.random.split(key, 1)
    shape = (2, TOKENS, VOCAB)
    return jnp.clip(3.0 * jax.random.normal(keys[0], shape), -18.0, 18.0).astype(jnp.bfloat16)


def draw_residual(key, part):
    key = jax.random.fold_in(key, 23)
    keys = jax.random.split(key, 1)
    column = jnp.arange(DT, dtype=jnp.float32)[None, :] / DT
    rising = 0.6 * jnp.exp(column * math.log(3.0))
    return (jnp.clip(jax.random.normal(keys[0], (TOKENS, DT)), -6.0, 6.0) * rising).astype(jnp.bfloat16)


def with_ends(entries, stream_key, least, largest):
    longest = entries.shape.index(max(entries.shape))
    spots = []
    for shift in (0, 1):
        where = [jax.random.randint(jax.random.fold_in(stream_key, axis), (), 0, length) for axis, length in enumerate(entries.shape)]
        where[longest] = (where[longest] + shift) % entries.shape[longest]
        spots.append(tuple(where))
    return entries.at[spots[0]].set(least).at[spots[1]].set(largest)


def strengthened(result, own_key, source, target, blocks, factor):
    def block_of(position):
        return (jnp.arange(result.shape[position]) // (result.shape[position] // blocks)).reshape((-1,) + (1,) * (result.ndim - 1 - position))

    one_side = jax.random.permutation(own_key, blocks)[block_of(target)]
    other_side = (block_of(target) + blocks // 2) % blocks
    return jnp.where((block_of(source) == one_side) | (block_of(source) == other_side), factor * result, result)


def level_of(stream_key, shape, cuts, low, high):
    def one(position, shards_of):
        draws = jax.random.uniform(jax.random.fold_in(jax.random.fold_in(stream_key, 6), position), (shards_of,), jnp.float32, low / len(cuts), high / len(cuts))
        return jnp.repeat(jnp.exp(draws), shape[position] // shards_of).reshape((-1,) + (1,) * (len(shape) - position - 1))

    gain = one(*cuts[0])
    for cut in cuts[1:]:
        gain = gain * one(*cut)
    return gain


def scatter_about(rng, dims, deviation, reach, cuts=(), held_as=jnp.bfloat16):
    entries = jax.random.normal(rng, dims, jnp.float32) * deviation
    if len(cuts) > 0:
        entries = level_of(rng, dims, cuts, -0.22, 0.18) * entries
    return jnp.clip(entries, min=-reach, max=reach).astype(held_as)


def gaussian_with(stream_key, extent, scale, bound, shards, heavy, kind=jnp.bfloat16):
    values = scale * jax.random.normal(stream_key, extent, jnp.float32)
    if shards:
        values = values * level_of(stream_key, extent, shards, -0.22, 0.18)
    return jnp.clip(strengthened(values, jax.random.fold_in(stream_key, 3), *heavy), -bound, bound).astype(kind)


def setup_inputs(seed: int = 0) -> dict:
    splits = jax.random.split(jax.random.key(seed), 9)
    hidden_pre = scatter_about(splits[0], (TOKENS, FF), 1.0, 6.0, ((0, 16), (1, 8)))
    residual = draw_residual(jax.random.fold_in(splits[8], 71), 0)
    w_down = scatter_about(splits[2], (DT, FF), FF ** -0.5, 0.0546875, ((0, 16), (1, 8)))
    head_weight = scatter_about(splits[3], (DT, VOCAB), DT ** -0.5, 0.109375, ((0, 16), (1, 8)))
    norm_gain = jnp.clip(1.0 + 0.1 * jax.random.normal(splits[4], (DT,), jnp.float32), 0.5, 1.5)
    segment_logits = draw_segment_logits(jax.random.fold_in(splits[8], 71), 0)
    student_hidden = gaussian_with(splits[6], (TOKENS, DS), 1.0, 24.0, ((0, 128),), (0, 1, 128, 5.5))
    frame_mask = with_ends((jax.random.randint(splits[7], (TOKENS,), 0, 4) < 3).astype(jnp.int32), jax.random.fold_in(splits[7], 1), 0, 1)
    return dict(hidden_pre=hidden_pre, residual=residual, w_down=w_down, head_weight=head_weight, norm_gain=norm_gain, segment_logits=segment_logits, student_hidden=student_hidden, frame_mask=frame_mask)


def reference(hidden_pre, residual, w_down, head_weight, norm_gain, segment_logits, student_hidden, frame_mask):
    active = jax.nn.silu(hidden_pre.astype(jnp.float32)).astype(jnp.bfloat16)
    share = FF // N_MP
    down_sum = jnp.zeros((TOKENS, DT), jnp.float32)
    for shard_index in range(N_MP):
        partial_term = lax.dot_general(active[:, shard_index * share:(shard_index + 1) * share], w_down[:, shard_index * share:(shard_index + 1) * share], (((1,), (1,)), ((), ())), preferred_element_type=jnp.float32)
        rounded = lax.optimization_barrier(partial_term.astype(jnp.bfloat16))
        down_sum = down_sum + rounded.astype(jnp.float32)
    middle = residual.astype(jnp.float32) + 0.5 * down_sum
    center = lax.optimization_barrier(jnp.mean(middle, axis=1, keepdims=True))
    spread = lax.optimization_barrier(jnp.mean(middle * middle, axis=1, keepdims=True)) - center * center
    normed = ((middle - center) * lax.rsqrt(spread + 1e-05) * norm_gain.astype(jnp.float32)).astype(jnp.bfloat16)
    next_logits = jnp.dot(normed, head_weight, preferred_element_type=jnp.float32).astype(jnp.bfloat16)
    teacher_post = jax.nn.softmax(segment_logits[0].astype(jnp.float32), axis=-1)
    student_post = jax.nn.softmax(segment_logits[1].astype(jnp.float32), axis=-1)
    logit_grad = (frame_mask.astype(jnp.float32)[:, None] * (student_post - teacher_post)).astype(jnp.bfloat16)
    weight_grad = lax.dot_general(student_hidden, logit_grad, (((0,), (0,)), ((), ())), preferred_element_type=jnp.float32)
    segment_out = jnp.stack([next_logits, logit_grad])
    grad_out = jnp.stack([jnp.zeros_like(weight_grad), weight_grad])
    return (segment_out, grad_out)
```

```python
import jax
import jax.numpy as jnp
from jax import lax
from jax.sharding import PartitionSpec as P

F32 = jnp.float32
BF16 = jnp.bfloat16
N_MP = 8


def dp_route(change):
    pairs = []
    for d in range(16):
        y, x, c = d // 8, (d // 2) % 4, d % 2
        y, x, c = change(y, x, c)
        pairs.append((d, y * 8 + (x % 4) * 2 + c))
    return pairs


X_UP = dp_route(lambda y, x, c: (y, x + 1, c))
X_DOWN = dp_route(lambda y, x, c: (y, x - 1, c))
Y_SWAP = dp_route(lambda y, x, c: (1 - y, x, c))
CORE_SWAP = dp_route(lambda y, x, c: (y, x, 1 - c))
Z_UP = [(i, (i + 1) % N_MP) for i in range(N_MP)]
Z_DOWN = [(i, (i - 1) % N_MP) for i in range(N_MP)]
SEC_SWAP = [(0, 1), (1, 0)]


def up(a):
    return lax.ppermute(a, "mp", Z_UP)


def down(a):
    return lax.ppermute(a, "mp", Z_DOWN)


def plus(a, b):
    return (a.astype(F32) + b.astype(F32)).astype(BF16)


def gather_x(block, x, core):
    rows, cols = block.shape
    half = rows // 2
    below = lax.ppermute(block, "dp", X_UP)
    above = lax.ppermute(block, "dp", X_DOWN)
    far_top = lax.ppermute(below[:half], "dp", X_UP)
    far_bottom = lax.ppermute(above[half:], "dp", X_DOWN)
    far = jnp.concatenate([far_top, far_bottom], axis=0)
    whole = jnp.zeros((8 * rows, cols), block.dtype)
    for shift, piece in ((0, block), (3, below), (1, above), (2, far)):
        place = ((x + shift) % 4) * 2
        other = lax.ppermute(piece, "dp", CORE_SWAP)
        whole = lax.dynamic_update_slice(whole, piece, ((place + core) * rows, 0))
        whole = lax.dynamic_update_slice(whole, other, ((place + 1 - core) * rows, 0))
    return whole


def scatter_sum_z(part, z):
    def own(k):
        return lax.dynamic_index_in_dim(part, (z + k) % N_MP, 0, keepdims=False)

    half = part.shape[1] // 2
    far = own(4)
    r = up(far[:half])
    l = down(far[half:])
    a, b = own(3), own(-3)
    r = up(jnp.concatenate([plus(a[:half], r), a[half:]], axis=0))
    l = down(jnp.concatenate([b[:half], plus(b[half:], l)], axis=0))
    r = up(plus(own(2), r))
    l = down(plus(own(-2), l))
    r = up(plus(own(1), r))
    l = down(plus(own(-1), l))
    return own(0).astype(F32) + r.astype(F32) + l.astype(F32)


def gather_z(block):
    half = block.shape[0] // 2
    r1, l1 = up(block), down(block)
    r2, l2 = up(r1), down(l1)
    r3, l3 = up(r2), down(l2)
    r4, l4 = up(r3[:half]), down(l3[half:])
    return [block, r1, l1, r2, l2, r3, l3, jnp.concatenate([r4, l4], axis=0)]


AWAY = (0, -1, 1, -2, 2, -3, 3, 4)


def body(
    hidden_pre, residual, w_down, head_weight, norm_gain, segment_logits, student_hidden, frame_mask
):
    s = lax.axis_index("sec")
    d = lax.axis_index("dp")
    z = lax.axis_index("mp")
    y, x, core = d // 8, (d // 2) % 4, d % 2
    frames = student_hidden.shape[0]
    half = frames // 2
    vocab = segment_logits.shape[2]

    rows = w_down.shape[0] // 2
    mine = lax.dynamic_slice_in_dim(w_down, s * rows, rows, 0)
    theirs = lax.ppermute(mine, "dp", Y_SWAP)
    active = jax.nn.silu(hidden_pre.astype(F32)).astype(BF16)
    sums = []
    for block in (mine, theirs):
        weights = gather_x(block, x, core)
        part = lax.dot_general(
            active, weights, (((1,), (1,)), ((), ())), preferred_element_type=F32
        ).astype(BF16)
        sums.append(scatter_sum_z(part.reshape(N_MP, frames, -1), z).astype(BF16))
    ordered = jnp.where(
        y == 0, jnp.concatenate(sums, axis=1), jnp.concatenate(sums[::-1], axis=1)
    )
    keep = lax.dynamic_slice_in_dim(ordered, s * half, half, 0)
    give = lax.dynamic_slice_in_dim(ordered, (1 - s) * half, half, 0)
    got = lax.ppermute(give, "sec", SEC_SWAP)
    down_sum = jnp.where(
        s == 0, jnp.concatenate([keep, got], axis=1), jnp.concatenate([got, keep], axis=1)
    ).astype(F32)

    blocks = residual.reshape(N_MP, 2, half, -1)
    blocks = lax.dynamic_index_in_dim(blocks, s, 1, keepdims=False)
    stream = lax.all_to_all(blocks, "mp", 0, 0, tiled=True)
    stream = stream.reshape(N_MP, half, 2, 2, rows).transpose(1, 3, 0, 2, 4).reshape(half, -1)
    gain = norm_gain.reshape(16, 2, rows).transpose(1, 0, 2).reshape(1, -1)
    head = lax.all_gather(head_weight.reshape(2, rows, -1), "dp", axis=1, tiled=False)
    head = head.reshape(-1, head_weight.shape[1])

    middle = stream.astype(F32) + 0.5 * down_sum
    center = jnp.mean(middle, axis=1, keepdims=True)
    spread = jnp.mean(middle * middle, axis=1, keepdims=True) - center * center
    normed = ((middle - center) * lax.rsqrt(spread + 1e-05) * gain).astype(BF16)
    every = jnp.concatenate(gather_z(normed), axis=0)
    logits = jnp.dot(every, head, preferred_element_type=F32).astype(BF16)
    logits = logits.reshape(N_MP, half, -1)
    lower = [None] * N_MP
    upper = [None] * N_MP
    for i, k in enumerate(AWAY):
        to = [(j, (j + k) % N_MP) for j in range(N_MP)]
        lower[-k % N_MP] = logits[i] if k == 0 else lax.ppermute(logits[i], "mp", to)
        upper[-k % N_MP] = lax.ppermute(
            logits[i], ("sec", "mp"), [(N_MP + a, b) for a, b in to]
        )
    turned = jnp.concatenate(
        [jnp.concatenate(lower, axis=1), jnp.concatenate(upper, axis=1)], axis=0
    )
    wide = turned.shape[1] // N_MP
    next_logits = lax.dynamic_slice_in_dim(
        jnp.concatenate([turned, turned], axis=1), ((N_MP - z) % N_MP) * wide, vocab, 1
    )

    own_logits = segment_logits[0]
    sent = lax.dynamic_slice_in_dim(own_logits, (1 - s) * half, half, 0)
    held = lax.dynamic_slice_in_dim(own_logits, s * half, half, 0)
    came = lax.ppermute(sent, "sec", SEC_SWAP)
    p_held = jax.nn.softmax(held.astype(F32), axis=-1)
    p_came = jax.nn.softmax(came.astype(F32), axis=-1)
    mask = lax.dynamic_slice_in_dim(frame_mask, s * half, half, 0).astype(F32)[:, None]
    sign = jnp.where(s == 0, -1.0, 1.0).astype(F32)
    grad = (mask * (sign * (p_held - p_came))).astype(BF16)
    grad_far = lax.ppermute(grad, "sec", [(0, 1)])
    hidden = lax.dynamic_slice_in_dim(student_hidden, s * half, half, 0)
    hidden = lax.all_gather(hidden, "dp", axis=0, tiled=True)
    cols = vocab // 16
    grad_cols = lax.all_to_all(
        grad.reshape(half, 16, cols).transpose(1, 0, 2), "dp", 0, 0, tiled=True
    ).reshape(16 * half, cols)
    product = lax.dot_general(
        hidden, grad_cols, (((0,), (0,)), ((), ())), preferred_element_type=F32
    )
    units = product.shape[0] // (16 * N_MP)
    product = product.reshape(16, N_MP, units, cols).transpose(1, 0, 2, 3)
    share = lax.psum_scatter(product, "mp", scatter_dimension=0, tiled=False)
    share = share + lax.ppermute(share, "sec", [(0, 1)])
    weight_grad = lax.all_to_all(share, "dp", 0, 0, tiled=True)
    weight_grad = weight_grad.transpose(1, 0, 2).reshape(units, vocab)

    is_teacher = s == 0
    segment = jnp.where(is_teacher, next_logits, jnp.concatenate([grad_far, grad], axis=0))
    return (segment[None], jnp.where(is_teacher, 0.0, weight_grad)[None])


def solution(mesh):
    placed = (
        P("dp", "mp"),
        P("dp", "mp"),
        P("dp", "mp"),
        P("dp", "mp"),
        P(),
        P("sec", ("dp", "mp"), None),
        P(("dp", "mp"), None),
        P(("dp", "mp")),
    )
    return jax.shard_map(
        body,
        mesh=mesh,
        in_specs=placed,
        out_specs=(P("sec", ("dp", "mp"), None), P("sec", ("dp", "mp"), None)),
        check_vma=False,
    )
```

```python
import jax
import jax.numpy as jnp
from jax import lax
from jax.experimental import pallas as pl
from jax.experimental.pallas import tpu as pltpu
from jax.sharding import Mesh, PartitionSpec as P

F32 = jnp.float32
BF16 = jnp.bfloat16
N_MP = 8
DP = ("yl", "x", "core")


def ring(n, k):
    return [(i, (i + k) % n) for i in range(n)]


def z_up(a):
    return lax.ppermute(a, "mp", ring(N_MP, 1))


def z_down(a):
    return lax.ppermute(a, "mp", ring(N_MP, -1))


def swap(a, axis):
    return lax.ppermute(a, axis, ring(2, 1))


def plus(a, b):
    return (a.astype(F32) + b.astype(F32)).astype(a.dtype)


def scatter_sum_z(part):
    half = part[4].shape[0] // 2
    r = z_up(part[4][:half])
    l = z_down(part[4][half:])
    a, b = part[3], part[5]
    r = z_up(jnp.concatenate([plus(a[:half], r), a[half:]], axis=0))
    l = z_down(jnp.concatenate([b[:half], plus(b[half:], l)], axis=0))
    r = z_up(plus(part[2], r))
    l = z_down(plus(part[6], l))
    passed = r
    r = z_up(plus(part[1], r))
    l = z_down(plus(part[7], l))
    return part[0].astype(F32) + r.astype(F32) + l.astype(F32), passed


def after(value, *earlier):
    ready = True
    for a in earlier:
        ready = ready & (a[(0,) * a.ndim].astype(F32) < 3e38)
    return jnp.where(ready, value, jnp.zeros_like(value))


def norm_kernel(place_ref, a_ref, b_ref, ga_ref, gb_ref, stream_ref, gain_ref, out_ref):
    s = place_ref[0]
    rows = a_ref.shape[1] // 8
    sums = [[], []]
    for own_ref, got_ref in ((a_ref, ga_ref), (b_ref, gb_ref)):
        own, got = own_ref[...].astype(F32), got_ref[...].astype(F32)
        sums[0].append(jnp.where(s == 0, own, got))
        sums[1].append(jnp.where(s == 0, got, own))
    pieces = []
    for d in range(16):
        at = (d % 8) * rows
        for sec in (0, 1):
            pieces.append(sums[sec][d // 8][:, at : at + rows])
    down_sum = jnp.concatenate(pieces, axis=1)
    stream = jnp.concatenate([stream_ref[m] for m in range(N_MP)], axis=1).astype(F32)
    middle = stream + 0.5 * down_sum
    center = jnp.mean(middle, axis=1, keepdims=True)
    spread = jnp.mean(middle * middle, axis=1, keepdims=True) - center * center
    normed = (middle - center) * lax.rsqrt(spread + 1e-05) * gain_ref[...]
    out_ref[...] = normed.astype(BF16)


def normalize(place, sums, got, stream, gain):
    frames = stream.shape[1]
    step = 32
    part = pl.BlockSpec((step, sums[0].shape[1]), lambda i, _: (i, 0))
    return pl.pallas_call(
        norm_kernel,
        grid_spec=pltpu.PrefetchScalarGridSpec(
            num_scalar_prefetch=1,
            grid=(frames // step,),
            in_specs=[
                part,
                part,
                part,
                part,
                pl.BlockSpec((N_MP, step, stream.shape[2]), lambda i, _: (0, i, 0)),
                pl.BlockSpec((1, gain.shape[1]), lambda i, _: (0, 0)),
            ],
            out_specs=pl.BlockSpec((step, gain.shape[1]), lambda i, _: (i, 0)),
        ),
        out_shape=jax.ShapeDtypeStruct((frames, gain.shape[1]), BF16),
        compiler_params=pltpu.CompilerParams(vmem_limit_bytes=24 * 1024 * 1024),
        name="normalize",
    )(place, *sums, *got, stream, gain)


def assemble_kernel(place_ref, logits_ref, far_ref, low_ref, high_ref, out_ref):
    teacher = place_ref[0] == 0
    wide = logits_ref.shape[1] // N_MP
    half = low_ref.shape[0]
    for m in range(N_MP):
        for part, ref in ((0, logits_ref), (1, far_ref)):
            at = pl.ds((2 * m + part) * wide, wide)
            for first, grad_ref in ((0, low_ref), (half, high_ref)):
                rows = pl.ds(first, half)
                out_ref[rows, at] = jnp.where(
                    teacher, ref[rows, pl.ds(m * wide, wide)], grad_ref[:, at]
                )


def assemble(place, logits, far, low, high):
    return pl.pallas_call(
        assemble_kernel,
        in_specs=[pl.BlockSpec(memory_space=pltpu.SMEM)]
        + [pl.BlockSpec(memory_space=pltpu.VMEM)] * 4,
        out_specs=pl.BlockSpec(memory_space=pltpu.VMEM),
        out_shape=jax.ShapeDtypeStruct((logits.shape[0], 2 * logits.shape[1]), BF16),
        compiler_params=pltpu.CompilerParams(vmem_limit_bytes=24 * 1024 * 1024),
        name="assemble",
    )(place.astype(jnp.int32), logits, far, low, high)


def body(
    hidden_pre, residual, w_down, head_weight, norm_gain, segment_logits, student_hidden, frame_mask
):
    s = lax.axis_index("sec")
    z = lax.axis_index("mp")
    frames = student_hidden.shape[0]
    half = frames // 2
    vocab = segment_logits.shape[2]
    rows = w_down.shape[0] // 2

    weights = lax.dynamic_slice_in_dim(w_down, s * rows, rows, 0)
    weights = lax.all_gather(weights, DP, axis=0, tiled=True)

    wide = head_weight.shape[1] // 2
    head = lax.dynamic_slice_in_dim(head_weight, s * wide, wide, 1)
    head = lax.all_to_all(
        jnp.broadcast_to(head[None], (N_MP,) + head.shape), "mp", 0, 0, tiled=True
    )
    head_part = head.transpose(1, 0, 2).reshape(-1, N_MP * wide)
    head = lax.all_gather(head_part, DP, axis=0, tiled=True)

    active = [
        lax.dynamic_slice_in_dim(hidden_pre, ((z + k) % N_MP) * frames, frames, 0)
        for k in range(N_MP)
    ]
    active[0] = after(active[0], head_part)
    active = jax.nn.silu(jnp.concatenate(active, axis=0).astype(F32)).astype(BF16)
    parts = [
        lax.dot_general(
            active, w, (((1,), (1,)), ((), ())), preferred_element_type=F32
        ).astype(BF16)
        for w in jnp.split(weights, 2, axis=0)
    ]
    sums, passed = zip(*[scatter_sum_z(p.reshape(N_MP, frames, -1)) for p in parts])
    sums = [a.astype(BF16) for a in sums]
    got = [swap(a, "sec") for a in sums]
    stream = lax.all_to_all(
        after(residual, head_part).reshape(N_MP, frames, -1), "mp", 0, 0, tiled=True
    )
    normed = normalize(s.reshape(1).astype(jnp.int32), sums, got, stream, norm_gain[None])
    logits = jnp.dot(normed, head, preferred_element_type=F32).astype(BF16)
    far = lax.ppermute(logits, "sec", [(1, 0)])
    own_logits = segment_logits[0]
    sent = lax.dynamic_slice_in_dim(own_logits, (1 - s) * half, half, 0)
    held = lax.dynamic_slice_in_dim(own_logits, s * half, half, 0)
    came = after(swap(sent, "sec"), parts[1])
    p_held = jax.nn.softmax(held.astype(F32), axis=-1)
    p_came = jax.nn.softmax(came.astype(F32), axis=-1)
    mask = lax.dynamic_slice_in_dim(frame_mask, s * half, half, 0).astype(F32)[:, None]
    sign = jnp.where(s == 0, -1.0, 1.0).astype(F32)
    grad = (mask * (sign * (p_held - p_came))).astype(BF16)
    grad_far = lax.ppermute(grad, "sec", [(0, 1)])
    hidden = lax.dynamic_slice_in_dim(student_hidden, s * half, half, 0)
    hidden = lax.all_to_all(
        jnp.broadcast_to(hidden[None], (16,) + hidden.shape), DP, 0, 0, tiled=True
    ).reshape(16 * half, -1)
    cols = vocab // 16
    grad_cols = lax.all_to_all(
        grad.reshape(half, 16, cols).transpose(1, 0, 2), DP, 0, 0, tiled=True
    ).reshape(16 * half, cols)
    grad_cols = after(grad_cols, grad_far, passed[0], passed[1])
    product = lax.dot_general(
        hidden, grad_cols, (((0,), (0,)), ((), ())), preferred_element_type=F32
    )
    units = product.shape[0] // (16 * N_MP)
    product = product.reshape(16, N_MP, units, cols)
    product = [
        lax.dynamic_index_in_dim(product, (z + k) % N_MP, 1, keepdims=False).reshape(-1, cols)
        for k in range(N_MP)
    ]
    share, _ = scatter_sum_z(product)
    share = after(share.reshape(16, units, cols), normed)
    share = share + lax.ppermute(share, "sec", [(0, 1)])
    weight_grad = lax.all_to_all(share, DP, 0, 0, tiled=True)
    weight_grad = weight_grad.transpose(1, 0, 2).reshape(units, vocab)

    is_teacher = s == 0
    segment = assemble(s.reshape(1), logits, far, grad_far, grad)
    return (segment[None], jnp.where(is_teacher, 0.0, weight_grad)[None])


def solution(mesh):
    fine = Mesh(mesh.devices.reshape(2, 2, 4, 2, N_MP), ("sec",) + DP + ("mp",))
    placed = (
        P(DP, "mp"),
        P(DP, "mp"),
        P(DP, "mp"),
        P(DP, "mp"),
        P(),
        P("sec", DP + ("mp",), None),
        P(DP + ("mp",), None),
        P(DP + ("mp",)),
    )
    return jax.shard_map(
        body,
        mesh=fine,
        in_specs=placed,
        out_specs=(P("sec", DP + ("mp",), None), P("sec", DP + ("mp",), None)),
        check_vma=False,
    )
```

```python
import jax
import jax.numpy as jnp
from jax import lax
from jax.experimental import pallas as pl
from jax.experimental.pallas import tpu as pltpu
from jax.sharding import Mesh, PartitionSpec as P

F32 = jnp.float32
BF16 = jnp.bfloat16
N_MP = 8
DP = ("yl", "x", "core")
TILES = ("core", "x", "yl")


def ring(n, k):
    return [(i, (i + k) % n) for i in range(n)]


def z_up(a):
    return lax.ppermute(a, "mp", ring(N_MP, 1))


def z_down(a):
    return lax.ppermute(a, "mp", ring(N_MP, -1))


def swap(a, axis):
    return lax.ppermute(a, axis, ring(2, 1))


def plus(a, b):
    return (a.astype(F32) + b.astype(F32)).astype(a.dtype)


def scatter_sum_z(part, late=()):
    half = part[4].shape[0] // 2
    r = z_up(part[4][:half])
    l = z_down(part[4][half:])
    a, b = part[3], part[5]
    r = z_up(jnp.concatenate([plus(a[:half], r), a[half:]], axis=0))
    l = z_down(jnp.concatenate([b[:half], plus(b[half:], l)], axis=0))
    r = z_up(plus(part[2], r))
    l = z_down(plus(part[6], l))
    r = z_up(plus(part[1], after(r, *late)))
    l = z_down(plus(part[7], l))
    return part[0].astype(F32) + r.astype(F32) + l.astype(F32)


def placed(pieces, rows):
    whole = jnp.zeros((rows, pieces[0][1].shape[1]), pieces[0][1].dtype)
    for at, piece in pieces:
        whole = lax.dynamic_update_slice(whole, piece, (at, 0))
    return whole


def gather_dp(block):
    rows = block.shape[0]
    y, x, core = (lax.axis_index(a) for a in ("yl", "x", "core"))
    pair = placed([(y * rows, block), ((1 - y) * rows, swap(block, "yl"))], 2 * rows)
    below = lax.ppermute(pair, "x", ring(4, 1))
    above = lax.ppermute(pair, "x", ring(4, -1))
    far_top = lax.ppermute(below[:rows], "x", ring(4, 1))
    far_bottom = lax.ppermute(above[rows:], "x", ring(4, -1))
    far = ((x + 2) % 4) * 2 * rows
    line = placed(
        [
            (x * 2 * rows, pair),
            (((x + 3) % 4) * 2 * rows, below),
            (((x + 1) % 4) * 2 * rows, above),
            (far, far_top),
            (far + rows, far_bottom),
        ],
        8 * rows,
    )
    other = swap(line, "core")
    return placed([(core * 8 * rows, line), ((1 - core) * 8 * rows, other)], 16 * rows)


AWAY = (0, -1, 1, -2, 2, -3, 3, 4)


def gather_z(block, third, fourth):
    half = block.shape[0] // 2
    r1, l1 = z_up(block), z_down(block)
    r2, l2 = z_up(r1), z_down(l1)
    r3, l3 = z_up(after(r2, third)), z_down(after(l2, third))
    r4, l4 = z_up(after(r3[:half], fourth)), z_down(after(l3[half:], fourth))
    return [block, r1, l1, r2, l2, r3, l3, jnp.concatenate([r4, l4], axis=0)]


def after(value, *earlier):
    ready = True
    for a in earlier:
        ready = ready & (a[(0,) * a.ndim].astype(F32) < 3e38)
    return jnp.where(ready, value, jnp.zeros_like(value))


def norm_kernel(place_ref, a_ref, b_ref, ga_ref, gb_ref, stream_ref, gain_ref, out_ref):
    s = place_ref[0]
    rows = a_ref.shape[1] // 8
    sums = [[], []]
    for own_ref, got_ref in ((a_ref, ga_ref), (b_ref, gb_ref)):
        own, got = own_ref[...].astype(F32), got_ref[...].astype(F32)
        sums[0].append(jnp.where(s == 0, own, got))
        sums[1].append(jnp.where(s == 0, got, own))
    pieces = []
    for d in range(16):
        at = (d % 8) * rows
        for sec in (0, 1):
            pieces.append(sums[sec][d // 8][:, at : at + rows])
    down_sum = jnp.concatenate(pieces, axis=1)
    stream = jnp.concatenate([stream_ref[m] for m in range(N_MP)], axis=1).astype(F32)
    middle = stream + 0.5 * down_sum
    center = jnp.mean(middle, axis=1, keepdims=True)
    spread = jnp.mean(middle * middle, axis=1, keepdims=True) - center * center
    normed = (middle - center) * lax.rsqrt(spread + 1e-05) * gain_ref[...]
    out_ref[...] = normed.astype(BF16)


def normalize(place, sums, got, stream, gain):
    frames = stream.shape[1]
    step = 32
    part = pl.BlockSpec((step, sums[0].shape[1]), lambda i, _: (i, 0))
    return pl.pallas_call(
        norm_kernel,
        grid_spec=pltpu.PrefetchScalarGridSpec(
            num_scalar_prefetch=1,
            grid=(frames // step,),
            in_specs=[
                part,
                part,
                part,
                part,
                pl.BlockSpec((N_MP, step, stream.shape[2]), lambda i, _: (0, i, 0)),
                pl.BlockSpec((1, gain.shape[1]), lambda i, _: (0, 0)),
            ],
            out_specs=pl.BlockSpec((step, gain.shape[1]), lambda i, _: (i, 0)),
        ),
        out_shape=jax.ShapeDtypeStruct((frames, gain.shape[1]), BF16),
        compiler_params=pltpu.CompilerParams(vmem_limit_bytes=24 * 1024 * 1024),
        name="normalize",
    )(place[:1], *sums, *got, stream, gain)


def assemble_kernel(place_ref, logits_ref, far_ref, low_ref, high_ref, out_ref):
    teacher = place_ref[0] == 0
    wide = logits_ref.shape[1] // N_MP
    half = low_ref.shape[0]
    for i, away in enumerate(AWAY):
        m = lax.rem(place_ref[1] + (away + N_MP), N_MP)
        for part, ref in ((0, logits_ref), (1, far_ref)):
            at = pl.ds(pl.multiple_of((2 * m + part) * wide, wide), wide)
            for first, grad_ref in ((0, low_ref), (half, high_ref)):
                rows = pl.ds(first, half)
                out_ref[rows, at] = jnp.where(
                    teacher, ref[rows, pl.ds(i * wide, wide)], grad_ref[:, at]
                )


def assemble(place, logits, far, low, high):
    return pl.pallas_call(
        assemble_kernel,
        in_specs=[pl.BlockSpec(memory_space=pltpu.SMEM)]
        + [pl.BlockSpec(memory_space=pltpu.VMEM)] * 4,
        out_specs=pl.BlockSpec(memory_space=pltpu.VMEM),
        out_shape=jax.ShapeDtypeStruct((logits.shape[0], 2 * logits.shape[1]), BF16),
        compiler_params=pltpu.CompilerParams(vmem_limit_bytes=24 * 1024 * 1024),
        name="assemble",
    )(place, logits, far, low, high)


def body(
    hidden_pre, residual, w_down, head_weight, norm_gain, segment_logits, student_hidden, frame_mask
):
    s = lax.axis_index("sec")
    z = lax.axis_index("mp")
    place = jnp.stack([s, z]).astype(jnp.int32)
    frames = student_hidden.shape[0]
    half = frames // 2
    vocab = segment_logits.shape[2]
    rows = w_down.shape[0] // 2

    weights = lax.dynamic_slice_in_dim(w_down, s * rows, rows, 0)
    weights = lax.all_gather(weights, DP, axis=0, tiled=True)

    own_logits = segment_logits[0]
    sent = lax.dynamic_slice_in_dim(own_logits, (1 - s) * half, half, 0)
    held = lax.dynamic_slice_in_dim(own_logits, s * half, half, 0)
    came = swap(sent, "sec")
    p_held = jax.nn.softmax(held.astype(F32), axis=-1)
    p_came = jax.nn.softmax(came.astype(F32), axis=-1)
    mask = lax.dynamic_slice_in_dim(frame_mask, s * half, half, 0).astype(F32)[:, None]
    sign = jnp.where(s == 0, -1.0, 1.0).astype(F32)
    grad = (mask * (sign * (p_held - p_came))).astype(BF16)
    wide = head_weight.shape[1] // 2
    head = lax.dynamic_slice_in_dim(head_weight, s * wide, wide, 1)
    hidden = gather_dp(lax.dynamic_slice_in_dim(student_hidden, s * half, half, 0))
    cols = vocab // 16
    to_dp = grad.reshape(half, 16, cols).transpose(1, 0, 2)
    head_part = jnp.concatenate(gather_z(head, came, to_dp), axis=1)
    head = lax.all_gather(head_part, DP, axis=0, tiled=True)

    stream = lax.all_to_all(
        after(residual, head_part).reshape(N_MP, frames, -1), "mp", 0, 0, tiled=True
    )
    grad_cols = lax.all_to_all(after(to_dp, stream), TILES, 0, 0, tiled=True).reshape(16 * half, cols)

    active = [
        lax.dynamic_slice_in_dim(hidden_pre, ((z + k) % N_MP) * frames, frames, 0)
        for k in range(N_MP)
    ]
    active[-1] = after(active[-1], head_part, grad_cols)
    active = jax.nn.silu(jnp.concatenate(active, axis=0).astype(F32)).astype(BF16)
    parts = [
        lax.dot_general(
            active, w, (((1,), (1,)), ((), ())), preferred_element_type=F32
        ).astype(BF16)
        for w in jnp.split(weights, 2, axis=0)
    ]
    grad_far = lax.ppermute(after(grad, parts[0]), "sec", [(0, 1)])
    product = lax.dot_general(
        hidden, grad_cols, (((0,), (0,)), ((), ())), preferred_element_type=F32
    ).astype(BF16)
    units = product.shape[0] // (16 * N_MP)
    product = product.reshape(2, 4, 2, N_MP, units, cols)
    first, second = (p.reshape(N_MP, frames, -1) for p in parts)
    joint = []
    for k in range(N_MP):
        block = lax.dynamic_index_in_dim(product, (z + k) % N_MP, 3, keepdims=False)
        block = block.transpose(2, 1, 0, 3, 4).reshape(frames, cols)
        joint.append(jnp.concatenate([second[k], block], axis=1))
    sums = [scatter_sum_z(first, (stream,)), scatter_sum_z(joint)]
    width = second.shape[2]
    share = sums[1][:, width:]
    sums = [a[:, :width].astype(BF16) for a in sums]
    got = [swap(a, "sec") for a in sums]
    normed = normalize(place, sums, got, stream, norm_gain[None])
    logits = jnp.dot(normed, head, preferred_element_type=F32).astype(BF16)
    far = lax.ppermute(logits, "sec", [(1, 0)])
    share = after(share.reshape(16, units, cols), grad_far)
    share = share + lax.ppermute(share, "sec", [(0, 1)])
    weight_grad = lax.all_to_all(share, TILES, 0, 0, tiled=True)
    weight_grad = weight_grad.transpose(1, 0, 2).reshape(units, vocab)

    is_teacher = s == 0
    segment = assemble(place, logits, far, grad_far, grad)
    return (segment[None], jnp.where(is_teacher, 0.0, weight_grad)[None])


def solution(mesh):
    fine = Mesh(mesh.devices.reshape(2, 2, 4, 2, N_MP), ("sec",) + DP + ("mp",))
    placed = (
        P(DP, "mp"),
        P(DP, "mp"),
        P(DP, "mp"),
        P(DP, "mp"),
        P(),
        P("sec", DP + ("mp",), None),
        P(DP + ("mp",), None),
        P(DP + ("mp",)),
    )
    return jax.shard_map(
        body,
        mesh=fine,
        in_specs=placed,
        out_specs=(P("sec", DP + ("mp",), None), P("sec", DP + ("mp",), None)),
        check_vma=False,
    )
```
